256 devices in a mesh: seq: 64 (over z, y, core), rep: 4 (over x).
Axes of the slice: x: 4, y: 4, z: 8, core: 2. Of those that a mesh axis runs over, the one named last changes fastest.
Arguments:
- query_rows: bfloat16 [98304, 1024], P(('seq', 'rep')), may hold values from -6 to 6
- key_rows: bfloat16 [98304, 128], P(('seq', 'rep')), may hold values from -6 to 6
- value_rows: bfloat16 [98304, 128], P(('seq', 'rep')), may hold values from -6 to 6
- out_grad: bfloat16 [98304, 1024], P(('seq', 'rep')), may hold values from -1.5 to 1.5
- logsumexp: float32 [8, 98304], P(None, ('seq', 'rep')), may hold values from 1 to 3
- row_delta: float32 [8, 98304], P(None, ('seq', 'rep')), may hold values from -8 to 8
- doc_lengths: int32 [255], replicated, may hold values from 1 to 1537, as said below
Outputs:
- query_grad: bfloat16 [98304, 1024], P(('seq', 'rep'))
- key_grad: bfloat16 [98304, 128], P(('seq', 'rep'))
- value_grad: bfloat16 [98304, 128], P(('seq', 'rep'))
The draws below stay inside these ranges and needn't reach their ends.
Inputs may be any that keep to these rules, and one draw needn't show every extreme that they name: `doc_lengths`: 255 document lengths in pack order, summing to 98304; so every document lies within 5 consecutive aligned blocks of 384 positions.
All inputs are finite; a program needn't handle non-finite values.
Results may differ from the reference program's by a relative error of at most 0.019.
Values may be sent and summed in bfloat16 or wider, within the bound.
No kernel may reach another device: no remote copies, remote signals or barrier semaphores. Data moves between devices by JAX's collectives and lax.ppermute only.
A program may use at most 64 MiB of HBM per device.

```python
import jax
import jax.numpy as jnp
from jax import lax

HEADS = 8
HD = 128
TOK_DEV = 384
REACH = 4
TOKENS = 98304
N_SEQ = 64
N_REP = 4


def draw_doc_lengths(key, part):
    blocks = N_SEQ * N_REP
    frames = 2 * blocks // REACH
    span = REACH * TOK_DEV // 2
    short_most = TOK_DEV // 4
    base_key = jax.random.fold_in(key, 11)
    key_start, key_short, key_pick = jax.random.split(base_key, 3)
    starts = jax.random.randint(key_start, (frames + 1,), short_most, span).astype(jnp.int32)
    shorts = jax.random.randint(key_short, (frames + 1,), 1, short_most + 1).astype(jnp.int32)
    chosen = jax.random.randint(key_pick, (), 1, frames - 1).astype(jnp.int32)
    index = jnp.arange(frames + 1, dtype=jnp.int32)
    starts = jnp.where(index == chosen + 1, span - 1, starts)
    starts = jnp.where(index == chosen - 1, jnp.minimum(starts, span - 4 - short_most), starts)
    starts = jnp.where(index == chosen, -3, starts)
    shorts = jnp.where(index == chosen + 1, 1, shorts)
    starts = jnp.where((index == 0) | (index == frames), 0, starts)
    long_start = index * span + starts
    short_start = long_start - shorts
    inner = jnp.stack([short_start[1:frames], long_start[1:frames]], 1).reshape(-1)
    bounds = jnp.concatenate([jnp.zeros((1,), jnp.int32), inner.astype(jnp.int32), jnp.full((1,), TOKENS, jnp.int32)])
    return (bounds[1:] - bounds[:-1]).astype(jnp.int32)


def block_levels(rng, shape, cuts, low, largest):
    def one(position, blocks):
        steps = jax.random.uniform(jax.random.fold_in(jax.random.fold_in(rng, 6), position), (blocks,), jnp.float32, low / len(cuts), largest / len(cuts))
        return jnp.repeat(jnp.exp(steps), shape[position] // blocks).reshape((-1,) + (1,) * (len(shape) - position - 1))

    gain = one(*cuts[0])
    for cut in cuts[1:]:
        gain = gain * one(*cut)
    return gain


def centred(key, dims, width, most, cuts=(), kind=jnp.bfloat16):
    values = width * jax.random.normal(key, dims, jnp.float32)
    if cuts:
        values = values * block_levels(key, dims, cuts, -0.22, 0.18)
    return jnp.clip(values, -most, most).astype(kind)


def setup_inputs(seed: int = 0) -> dict:
    seeds = jax.random.split(jax.random.key(seed), 8)
    query_rows = centred(seeds[0], (TOKENS, HEADS * HD), 1.0, 6.0, ((0, 256),))
    key_rows = centred(seeds[1], (TOKENS, HD), 1.0, 6.0, ((0, 256),))
    value_rows = centred(seeds[2], (TOKENS, HD), 1.0, 6.0, ((0, 256),))
    out_grad = centred(seeds[3], (TOKENS, HEADS * HD), 0.25, 1.5, ((0, 256),))
    logsumexp = jnp.clip(1.0 + 2.0 * jax.random.uniform(seeds[4], (HEADS, TOKENS), jnp.float32) ** block_levels(seeds[4], (HEADS, TOKENS), ((1, 256),), -0.2, 0.2), 1.0, 3.0)
    row_delta = centred(seeds[5], (HEADS, TOKENS), 2.0, 8.0, ((1, 256),), jnp.float32)
    doc_lengths = draw_doc_lengths(jax.random.fold_in(seeds[7], 71), 0)
    return {"query_rows": query_rows, "key_rows": key_rows, "value_rows": value_rows, "out_grad": out_grad, "logsumexp": logsumexp, "row_delta": row_delta, "doc_lengths": doc_lengths}


def block_grads(query_block, grad_block, stat_block, delta_block, key_block, value_block, query_docs, key_docs, query_pos, key_pos):
    row_count = query_block.shape[0]
    query_heads = query_block.astype(jnp.float32).reshape(row_count, HEADS, HD)
    grad_heads = grad_block.astype(jnp.float32).reshape(row_count, HEADS, HD)
    key_float = key_block.astype(jnp.float32)
    value_float = value_block.astype(jnp.float32)
    score_scale = HD ** -0.5
    scores = jnp.einsum("qhd,kd->hqk", query_heads, key_float) * score_scale
    allowed = (query_docs[:, None] == key_docs[None, :]) & (key_pos[None, :] <= query_pos[:, None])
    probs = jnp.where(allowed[None], jnp.exp(scores - stat_block[:, :, None]), 0.0)
    dprobs = jnp.einsum("qhd,kd->hqk", grad_heads, value_float)
    dscores = probs * (dprobs - delta_block[:, :, None])
    probs_half = probs.astype(jnp.bfloat16).astype(jnp.float32)
    dscores_half = dscores.astype(jnp.bfloat16).astype(jnp.float32)
    query_part = (jnp.einsum("hqk,kd->qhd", dscores_half, key_float) * score_scale).reshape(row_count, HEADS * HD)
    key_part = jnp.einsum("hqk,qhd->kd", dscores_half, query_heads) * score_scale
    value_part = jnp.einsum("hqk,qhd->kd", probs_half, grad_heads)
    return query_part, key_part, value_part


def shifted_blocks(array, distance, filler):
    return jnp.concatenate([filler, array[:-distance]], 0)


def reference(query_rows, key_rows, value_rows, out_grad, logsumexp, row_delta, doc_lengths):
    blocks = N_SEQ * N_REP
    total = blocks * TOK_DEV
    doc_ends = jnp.cumsum(doc_lengths).astype(jnp.int32)
    marks = jnp.zeros((total,), jnp.int32).at[doc_ends[:-1]].add(1)
    docs = jnp.cumsum(marks).astype(jnp.int32).reshape(blocks, TOK_DEV)
    positions = jnp.arange(total, dtype=jnp.int32).reshape(blocks, TOK_DEV)
    queries = query_rows.reshape(blocks, TOK_DEV, HEADS * HD)
    grads = out_grad.reshape(blocks, TOK_DEV, HEADS * HD)
    keys_all = key_rows.reshape(blocks, TOK_DEV, HD)
    values_all = value_rows.reshape(blocks, TOK_DEV, HD)
    stats = logsumexp.reshape(HEADS, blocks, TOK_DEV).transpose(1, 0, 2)
    deltas = row_delta.reshape(HEADS, blocks, TOK_DEV).transpose(1, 0, 2)
    prev_keys = jnp.stack([shifted_blocks(keys_all, step, jnp.zeros_like(keys_all[:step])) for step in range(1, REACH + 1)], 1)
    prev_values = jnp.stack([shifted_blocks(values_all, step, jnp.zeros_like(values_all[:step])) for step in range(1, REACH + 1)], 1)
    prev_docs = jnp.stack([shifted_blocks(docs, step, jnp.full((step, TOK_DEV), -1, jnp.int32)) for step in range(1, REACH + 1)], 1)
    prev_pos = jnp.stack([positions - step * TOK_DEV for step in range(1, REACH + 1)], 1)

    def one_block(block_items):
        query_block, grad_block, stat_block, delta_block, key_block, value_block, doc_block, pos_block, pkey, pvalue, pdoc, ppos = block_items
        query_sum, local_k, local_v = block_grads(query_block, grad_block, stat_block, delta_block, key_block, value_block, doc_block, doc_block, pos_block, pos_block)
        cross_keys = []
        cross_values = []
        for step in range(REACH):
            cross_q, cross_k, cross_v = block_grads(query_block, grad_block, stat_block, delta_block, pkey[step], pvalue[step], doc_block, pdoc[step], pos_block, ppos[step])
            query_sum = query_sum + cross_q
            cross_keys.append(cross_k)
            cross_values.append(cross_v)
        return query_sum, local_k, local_v, jnp.stack(cross_keys, 0), jnp.stack(cross_values, 0)

    query_sum, local_k, local_v, cross_k, cross_v = lax.map(one_block, (queries, grads, stats, deltas, keys_all, values_all, docs, positions, prev_keys, prev_values, prev_docs, prev_pos))
    key_sum = local_k
    value_sum = local_v
    for step in range(1, REACH + 1):
        key_sum = key_sum + jnp.concatenate([cross_k[step:, step - 1], jnp.zeros_like(cross_k[:step, step - 1])], 0)
        value_sum = value_sum + jnp.concatenate([cross_v[step:, step - 1], jnp.zeros_like(cross_v[:step, step - 1])], 0)
    return (query_sum.reshape(total, HEADS * HD).astype(jnp.bfloat16), key_sum.reshape(total, HD).astype(jnp.bfloat16), value_sum.reshape(total, HD).astype(jnp.bfloat16))
```

```python
import functools

import jax
import jax.numpy as jnp
from jax import lax
from jax.experimental import pallas as pl
from jax.experimental.pallas import tpu as pltpu
from jax.sharding import PartitionSpec as P

AXES = ("seq", "rep")
REACH = 4
HEADS = 8
HD = 128
TOK = 384
SCALE = HD**-0.5
LOG2E = 1.4426950408889634
FAR = 1e30

NT = (((1,), (1,)), ((), ()))
NN = (((1,), (0,)), ((), ()))
VM = pl.BlockSpec(memory_space=pltpu.VMEM)
SM = pl.BlockSpec(memory_space=pltpu.SMEM)


def dot(a, b, dims):
    return lax.dot_general(a, b, dims, preferred_element_type=jnp.float32)


def shift(array, by):
    length = lax.axis_size(AXES)
    pairs = [(i, i + by) for i in range(length) if 0 <= i + by < length]
    return lax.ppermute(array, AXES, pairs)


def prep_kernel(first_ref, lengths_ref, starts_ref):
    count = lengths_ref.shape[1]
    row = lax.broadcasted_iota(jnp.int32, (count, count), 0)
    col = lax.broadcasted_iota(jnp.int32, (count, count), 1)
    ends = jnp.sum(jnp.where(col <= row, lengths_ref[...], 0), axis=1, keepdims=True)
    first = first_ref[0]
    pos = first + lax.broadcasted_iota(jnp.int32, (1, TOK), 1)
    starts_ref[...] = jnp.max(jnp.where(ends <= pos, ends, 0), axis=0, keepdims=True) - first


def cross_kernel(distance, q, g, lse, delta, starts, kv, dq_in, dq, dkv, ps, dss):
    begin = starts[...]
    shared = begin <= 0
    key0 = jnp.max(jnp.where(lax.broadcasted_iota(jnp.int32, (1, TOK), 1) == 0, begin, -(2**30))) + TOK * distance

    def part(low):
        rows = TOK - low
        at = lax.broadcasted_iota(jnp.int32, (rows, 1), 0) + low
        live = at >= key0
        key = jnp.where(live, kv[low:, :HD], 0)
        value = jnp.where(live, kv[low:, HD:], 0)
        key_t = key.T
        for h in range(HEADS):
            hd = slice(h * HD, (h + 1) * HD)
            ht = slice(h * TOK, (h + 1) * TOK)
            l2 = jnp.where(shared, lse[h : h + 1, :] * LOG2E, FAR)
            s = dot(key, q[:, hd], NT)
            p = jnp.exp2(s * (SCALE * LOG2E) - l2)
            ds = p * (dot(value, g[:, hd], NT) - delta[h : h + 1, :])
            ps[low:, ht] = p.astype(jnp.bfloat16)
            dss[low:, ht] = ds.astype(jnp.bfloat16)
        for h in range(HEADS):
            ht = slice(h * TOK, (h + 1) * TOK)
            dq[h] = dq_in[h] + dot(key_t, dss[low:, ht], NN)
        dk = dv = None
        for h in range(HEADS):
            hd = slice(h * HD, (h + 1) * HD)
            ht = slice(h * TOK, (h + 1) * TOK)
            a = dot(ps[low:, ht], g[:, hd], NN)
            b = dot(dss[low:, ht], q[:, hd], NN)
            dv = a if dv is None else dv + a
            dk = b if dk is None else dk + b
        if low:
            dkv[:low, :] = jnp.zeros((low, 2 * HD), dkv.dtype)
        dkv[low:, :HD] = jnp.where(live, dk * SCALE, 0.0).astype(dkv.dtype)
        dkv[low:, HD:] = jnp.where(live, dv, 0.0).astype(dkv.dtype)

    @pl.when(key0 >= TOK)
    def _():
        dkv[...] = jnp.zeros_like(dkv)
        dq[...] = dq_in[...]

    @pl.when((key0 < TOK) & (key0 >= TOK - 128))
    def _():
        part(TOK - 128)

    @pl.when(key0 < TOK - 128)
    def _():
        part(0)


def own_kernel(q, g, lse, delta, starts, kv, dq, dkv, bias, ps, dss):
    begin = starts[...]
    at = lax.broadcasted_iota(jnp.int32, (TOK, TOK), 0)
    to = lax.broadcasted_iota(jnp.int32, (TOK, TOK), 1)
    bias[...] = jnp.where((at <= to) & (at >= begin), 0.0, -FAR)
    for j in range(0, TOK, 128):
        key = kv[j : j + 128, :HD]
        value = kv[j : j + 128, HD:]
        key_t = key.T
        for h in range(HEADS):
            hd = slice(h * HD, (h + 1) * HD)
            ht = slice(h * TOK + j, (h + 1) * TOK)
            s = dot(key, q[j:, hd], NT)
            p = jnp.exp2(s * (SCALE * LOG2E) - lse[h : h + 1, j:] * LOG2E + bias[j : j + 128, j:])
            ds = p * (dot(value, g[j:, hd], NT) - delta[h : h + 1, j:])
            ps[j : j + 128, ht] = p.astype(jnp.bfloat16)
            dss[j : j + 128, ht] = ds.astype(jnp.bfloat16)
    for j in range(0, TOK, 128):
        key_t = kv[: j + 128, :HD].T
        for h in range(HEADS):
            ht = slice(h * TOK + j, h * TOK + j + 128)
            dq[h, :, j : j + 128] = dot(key_t, dss[: j + 128, ht], NN)
    for j in range(0, TOK, 128):
        dk = dv = None
        for h in range(HEADS):
            hd = slice(h * HD, (h + 1) * HD)
            ht = slice(h * TOK + j, (h + 1) * TOK)
            a = dot(ps[j : j + 128, ht], g[j:, hd], NN)
            b = dot(dss[j : j + 128, ht], q[j:, hd], NN)
            dv = a if dv is None else dv + a
            dk = b if dk is None else dk + b
        dkv[j : j + 128, :HD] = dk * SCALE
        dkv[j : j + 128, HD:] = dv


def finish_kernel(dq, own, b1, b2, b3, b4, dq_out, dk_out, dv_out):
    for h in range(HEADS):
        dq_out[:, h * HD : (h + 1) * HD] = (dq[h] * SCALE).T.astype(dq_out.dtype)
    total = own[...]
    for b in (b1, b2, b3, b4):
        total = total + b[...].astype(jnp.float32)
    dk_out[...] = total[:, :HD].astype(dk_out.dtype)
    dv_out[...] = total[:, HD:].astype(dv_out.dtype)


def params(**more):
    return pltpu.CompilerParams(vmem_limit_bytes=24 << 20, **more)


def cost(flops):
    return pl.CostEstimate(flops=flops, bytes_accessed=4 << 20, transcendentals=0)


PAIR = 10 * HEADS * TOK * TOK * HD


def shards(query_rows, key_rows, value_rows, out_grad, logsumexp, row_delta, doc_lengths):
    bf, f32 = jnp.bfloat16, jnp.float32
    first = (lax.axis_index(AXES) * TOK).astype(jnp.int32).reshape(1)
    kv = jnp.concatenate([key_rows, value_rows], 1)
    arrived = {d: shift(kv, d) for d in (1, 2, 3, 4)}
    starts = pl.pallas_call(
        prep_kernel,
        out_shape=jax.ShapeDtypeStruct((1, TOK), jnp.int32),
        in_specs=[SM, VM],
        out_specs=VM,
        compiler_params=params(),
        name="prep",
    )(first, doc_lengths.reshape(1, -1))
    dq_shape = jax.ShapeDtypeStruct((HEADS, HD, TOK), f32)
    half = pltpu.VMEM((TOK, HEADS * TOK), bf)
    dq, own = pl.pallas_call(
        own_kernel,
        out_shape=[dq_shape, jax.ShapeDtypeStruct((TOK, 2 * HD), f32)],
        in_specs=[VM] * 6,
        out_specs=[VM] * 2,
        scratch_shapes=[pltpu.VMEM((TOK, TOK), f32), half, half],
        compiler_params=params(),
        cost_estimate=cost(PAIR),
        name="own",
    )(query_rows, out_grad, logsumexp, row_delta, starts, kv)
    returned = {}
    for d in (1, 2, 3, 4):
        dq, part = pl.pallas_call(
            functools.partial(cross_kernel, d),
            out_shape=[dq_shape, jax.ShapeDtypeStruct((TOK, 2 * HD), bf)],
            in_specs=[VM] * 7,
            out_specs=[VM] * 2,
            scratch_shapes=[half, half],
            input_output_aliases={6: 0},
            compiler_params=params(),
            cost_estimate=cost(PAIR),
            name=f"cross{d}",
        )(query_rows, out_grad, logsumexp, row_delta, starts, arrived[d], dq)
        returned[d] = shift(part, -d)
    return pl.pallas_call(
        finish_kernel,
        out_shape=[
            jax.ShapeDtypeStruct((TOK, HEADS * HD), bf),
            jax.ShapeDtypeStruct((TOK, HD), bf),
            jax.ShapeDtypeStruct((TOK, HD), bf),
        ],
        in_specs=[VM] * 6,
        out_specs=[VM] * 3,
        compiler_params=params(),
        name="finish",
    )(dq, own, *[returned[d] for d in (1, 2, 3, 4)])


def solution(mesh):
    rows = P(AXES, None)
    return jax.shard_map(
        shards,
        mesh=mesh,
        in_specs=(rows, rows, rows, rows, P(None, AXES), P(None, AXES), P()),
        out_specs=(rows, rows, rows),
        check_vma=False,
    )
```

```python
import functools

import jax
import jax.numpy as jnp
from jax import lax
from jax.experimental import pallas as pl
from jax.experimental.pallas import tpu as pltpu
from jax.sharding import PartitionSpec as P

AXES = ("seq", "rep")
REACH = 4
HEADS = 8
HD = 128
TOK = 384
TILE = 128
WIDE = HEADS * TILE
SCALE = HD**-0.5
LOG2E = 1.4426950408889634
FAR = 1e30

NT = (((1,), (1,)), ((), ()))
NN = (((1,), (0,)), ((), ()))
VM = pl.BlockSpec(memory_space=pltpu.VMEM)
SM = pl.BlockSpec(memory_space=pltpu.SMEM)
ANY = pl.BlockSpec(memory_space=pl.ANY)
HB = pl.BlockSpec(memory_space=pltpu.HBM)


def dot(a, b, dims):
    return lax.dot_general(a, b, dims, preferred_element_type=jnp.float32)


def hbm(array):
    return pltpu.with_memory_space_constraint(array, pltpu.HBM)


def vmem(like):
    return pltpu.VMEM(like.shape, like.dtype)


def shift(array, by):
    length = lax.axis_size(AXES)
    pairs = [(i, i + by) for i in range(length) if 0 <= i + by < length]
    return lax.ppermute(array, AXES, pairs)


def pack_kernel(key, value, kv, sem):
    copies = [
        pltpu.make_async_copy(key, kv.at[:, :HD], sem.at[0]),
        pltpu.make_async_copy(value, kv.at[:, HD:], sem.at[1]),
    ]
    for copy in copies:
        copy.start()
    for copy in copies:
        copy.wait()


def cross_kernel(distance, q, g, lse, delta, starts, kv, dq_in, after, dq, dkv, held, acc):
    begin = starts[...]
    lane = lax.broadcasted_iota(jnp.int32, (1, TOK), 1)
    key0 = jnp.max(jnp.where(lane == 0, begin, -(2**30))) + TOK * distance
    tiles = (jnp.sum((begin <= 0).astype(jnp.int32)) + TILE - 1) // TILE

    def part(low):
        key = held[low:, :HD]
        value = held[low:, HD:]
        key_t = key.T

        def step(n, carry):
            at = pl.ds(pl.multiple_of(n * WIDE, WIDE), WIDE)
            s = dot(key, q[at, :], NT)
            p = jnp.exp2(s * (SCALE * LOG2E) - lse[:, at])
            ds = p * (dot(value, g[at, :], NT) - delta[:, at])
            p = p.astype(jnp.bfloat16)
            ds = ds.astype(jnp.bfloat16)
            dq[:, at] = dq_in[:, at] + dot(key_t, ds, NN)
            acc[low:, :HD] += dot(ds, q[at, :], NN)
            acc[low:, HD:] += dot(p, g[at, :], NN)
            return carry

        lax.fori_loop(0, tiles, step, 0)

    @pl.when(key0 >= TOK)
    def _():
        dkv[...] = jnp.zeros_like(dkv)

    @pl.when(key0 < TOK)
    def _():
        live = lax.broadcasted_iota(jnp.int32, (TOK, 1), 0) >= key0
        held[...] = jnp.where(live, kv[...], 0)
        acc[...] = jnp.zeros_like(acc)
        for low in range(0, TOK, TILE):
            reached = key0 < low + TILE
            if low:
                reached &= key0 >= low

            @pl.when(reached)
            def _(low=low):
                part(low)

        dkv[:, :HD] = jnp.where(live, acc[:, :HD] * SCALE, 0.0).astype(dkv.dtype)
        dkv[:, HD:] = jnp.where(live, acc[:, HD:], 0.0).astype(dkv.dtype)


def own_kernel(first_ref, lengths, q, g, lse, delta, kv, *refs):
    starts, qs, gs, own_lse, far_lse, row_delta, dq, dkv, again, bias = refs
    again[...] = kv[...]
    count = lengths.shape[1]
    row = lax.broadcasted_iota(jnp.int32, (count, count), 0)
    col = lax.broadcasted_iota(jnp.int32, (count, count), 1)
    ends = jnp.sum(jnp.where(col <= row, lengths[...], 0), axis=1, keepdims=True)
    first = first_ref[0]
    pos = first + lax.broadcasted_iota(jnp.int32, (1, TOK), 1)
    begin = jnp.max(jnp.where(ends <= pos, ends, 0), axis=0, keepdims=True) - first
    starts[...] = begin
    at = lax.broadcasted_iota(jnp.int32, (TOK, TOK), 0)
    to = lax.broadcasted_iota(jnp.int32, (TOK, TOK), 1)
    bias[...] = jnp.where((at <= to) & (at >= begin), 0.0, -FAR)
    dkv[...] = jnp.zeros_like(dkv)
    for n in range(TOK // TILE):
        rows = slice(n * TILE, (n + 1) * TILE)
        wide = slice(n * WIDE, (n + 1) * WIDE)
        high = (n + 1) * TILE
        for h in range(HEADS):
            hd = slice(h * HD, (h + 1) * HD)
            to = slice(n * WIDE + h * TILE, n * WIDE + (h + 1) * TILE)
            qs[to, :] = q[rows, hd]
            gs[to, :] = g[rows, hd]
            l2 = lse[h : h + 1, rows] * LOG2E
            own_lse[:, to] = l2
            far_lse[:, to] = jnp.where(begin[:, rows] <= 0, l2, FAR)
            row_delta[:, to] = delta[h : h + 1, rows]
        key = kv[:high, :HD]
        mask = jnp.concatenate([bias[:high, rows]] * HEADS, axis=1)
        s = dot(key, qs[wide, :], NT)
        p = jnp.exp2(s * (SCALE * LOG2E) - own_lse[:, wide] + mask)
        ds = p * (dot(kv[:high, HD:], gs[wide, :], NT) - row_delta[:, wide])
        p = p.astype(jnp.bfloat16)
        ds = ds.astype(jnp.bfloat16)
        dq[:, wide] = dot(key.T, ds, NN)
        dkv[:high, :HD] += dot(ds, qs[wide, :], NN)
        dkv[:high, HD:] += dot(p, gs[wide, :], NN)
    dkv[:, :HD] = dkv[:, :HD] * SCALE


def turn_kernel(dq, *refs):
    dq_out = refs[-1]
    for n in range(TOK // TILE):
        for h in range(HEADS):
            block = dq[:, n * WIDE + h * TILE : n * WIDE + (h + 1) * TILE]
            dq_out[n * TILE : (n + 1) * TILE, h * HD : (h + 1) * HD] = (block * SCALE).T.astype(dq_out.dtype)


def finish_kernel(own, b1, b2, b3, b4, dk_out, dv_out):
    total = own[...]
    for b in (b1, b2, b3, b4):
        total = total + b[...].astype(jnp.float32)
    dk_out[...] = total[:, :HD].astype(dk_out.dtype)
    dv_out[...] = total[:, HD:].astype(dv_out.dtype)


def params(**more):
    return pltpu.CompilerParams(vmem_limit_bytes=24 << 20, **more)


EARLY = (1, 4)
LATE = (3, 2)
ORDER = (1, 3, 2, 4)
LAG = 3
COST = pl.CostEstimate(flops=2000000000, bytes_accessed=0, transcendentals=0)
FIRST = pl.CostEstimate(flops=10**10, bytes_accessed=0, transcendentals=0)


def shards(query_rows, key_rows, value_rows, out_grad, logsumexp, row_delta, doc_lengths):
    bf, f32 = jnp.bfloat16, jnp.float32
    shape = jax.ShapeDtypeStruct
    first = (lax.axis_index(AXES) * TOK).astype(jnp.int32).reshape(1)
    kv = pl.pallas_call(
        pack_kernel,
        out_shape=vmem(shape((TOK, 2 * HD), bf)),
        in_specs=[HB] * 2,
        out_specs=VM,
        scratch_shapes=[pltpu.SemaphoreType.DMA((2,))],
        compiler_params=params(),
        cost_estimate=FIRST,
        name="pack",
    )(hbm(key_rows), hbm(value_rows))
    arrived = {d: shift(kv, d) for d in EARLY}
    dq_shape = shape((HD, HEADS * TOK), f32)
    row = vmem(shape((1, HEADS * TOK), f32))
    starts, query, grad, own_lse, lse, delta, dq, own, again = pl.pallas_call(
        own_kernel,
        out_shape=[
            vmem(shape((1, TOK), jnp.int32)),
            vmem(shape((HEADS * TOK, HD), bf)),
            vmem(shape((HEADS * TOK, HD), bf)),
            row,
            row,
            row,
            vmem(dq_shape),
            vmem(shape((TOK, 2 * HD), f32)),
            vmem(shape((TOK, 2 * HD), bf)),
        ],
        in_specs=[SM] + [VM] * 6,
        out_specs=[VM] * 9,
        scratch_shapes=[pltpu.VMEM((TOK, TOK), f32)],
        compiler_params=params(),
        cost_estimate=COST,
        name="own",
    )(first, doc_lengths.reshape(1, -1), query_rows, out_grad, logsumexp, row_delta, kv)
    for d in LATE:
        arrived[d] = shift(again, d)
    returned = {}
    for n, d in enumerate(ORDER):
        after = returned[ORDER[n - LAG]] if n >= LAG else starts
        dq, part = pl.pallas_call(
            functools.partial(cross_kernel, d),
            out_shape=[vmem(dq_shape), vmem(shape((TOK, 2 * HD), bf))],
            in_specs=[VM] * 7 + [ANY],
            out_specs=[VM] * 2,
            scratch_shapes=[pltpu.VMEM((TOK, 2 * HD), bf), pltpu.VMEM((TOK, 2 * HD), f32)],
            input_output_aliases={6: 0},
            compiler_params=params(),
            cost_estimate=COST,
            name=f"cross{d}",
        )(query, grad, lse, delta, starts, arrived[d], dq, after)
        returned[d] = shift(part, -d)
    tokens = [returned[d] for d in ORDER[4 - LAG : 3]]
    query_grad = pl.pallas_call(
        turn_kernel,
        out_shape=shape((TOK, HEADS * HD), bf),
        in_specs=[VM] + [ANY] * len(tokens),
        out_specs=VM,
        compiler_params=params(),
        cost_estimate=COST,
        name="turn",
    )(dq, *tokens)
    key_grad, value_grad = pl.pallas_call(
        finish_kernel,
        out_shape=[shape((TOK, HD), bf)] * 2,
        in_specs=[VM] * 5,
        out_specs=[VM] * 2,
        compiler_params=params(),
        cost_estimate=COST,
        name="finish",
    )(own, *[returned[d] for d in ORDER])
    return query_grad, key_grad, value_grad


def solution(mesh):
    rows = P(AXES, None)
    return jax.shard_map(
        shards,
        mesh=mesh,
        in_specs=(rows, rows, rows, rows, P(None, AXES), P(None, AXES), P()),
        out_specs=(rows, rows, rows),
        check_vma=False,
    )
```

```python
import functools

import jax
import jax.numpy as jnp
from jax import lax
from jax.experimental import pallas as pl
from jax.experimental.pallas import tpu as pltpu
from jax.sharding import PartitionSpec as P

AXES = ("seq", "rep")
REACH = 4
HEADS = 8
HD = 128
TOK = 384
TILE = 128
WIDE = HEADS * TILE
SCALE = HD**-0.5
LOG2E = 1.4426950408889634
FAR = 1e30

NT = (((1,), (1,)), ((), ()))
NN = (((1,), (0,)), ((), ()))
VM = pl.BlockSpec(memory_space=pltpu.VMEM)
SM = pl.BlockSpec(memory_space=pltpu.SMEM)
ANY = pl.BlockSpec(memory_space=pl.ANY)
HB = pl.BlockSpec(memory_space=pltpu.HBM)


def dot(a, b, dims):
    return lax.dot_general(a, b, dims, preferred_element_type=jnp.float32)


def hbm(array):
    return pltpu.with_memory_space_constraint(array, pltpu.HBM)


def vmem(like):
    return pltpu.VMEM(like.shape, like.dtype)


def shift(array, by):
    length = lax.axis_size(AXES)
    pairs = [(i, i + by) for i in range(length) if 0 <= i + by < length]
    return lax.ppermute(array, AXES, pairs)


def pack_kernel(key, value, kv, sem):
    copies = [
        pltpu.make_async_copy(key, kv.at[:, :HD], sem.at[0]),
        pltpu.make_async_copy(value, kv.at[:, HD:], sem.at[1]),
    ]
    for copy in copies:
        copy.start()
    for copy in copies:
        copy.wait()


def cross_kernel(distances, extra, q, g, lse, delta, starts, *refs):
    count = len(distances)
    blocks, dq_in = refs[:count], refs[count]
    dq, *outs = refs[count + 1 + extra : -2]
    held, acc = refs[-2:]
    begin = starts[...]
    lane = lax.broadcasted_iota(jnp.int32, (1, TOK), 1)
    reach = jnp.max(jnp.where(lane == 0, begin, -(2**30)))
    tiles = (jnp.sum((begin <= 0).astype(jnp.int32)) + TILE - 1) // TILE

    def part(low):
        key = held[low:, :HD]
        value = held[low:, HD:]
        key_t = key.T

        def step(n, carry):
            at = pl.ds(pl.multiple_of(n * WIDE, WIDE), WIDE)
            s = dot(key, q[at, :], NT)
            p = jnp.exp2(s * (SCALE * LOG2E) - lse[:, at])
            ds = p * (dot(value, g[at, :], NT) - delta[:, at])
            p = p.astype(jnp.bfloat16)
            ds = ds.astype(jnp.bfloat16)
            dq[:, at] = dq_in[:, at] + dot(key_t, ds, NN)
            acc[low:, :HD] += dot(ds, q[at, :], NN)
            acc[low:, HD:] += dot(p, g[at, :], NN)
            return carry

        lax.fori_loop(0, tiles, step, 0)

    for distance, kv, dkv in zip(distances, blocks, outs):
        key0 = reach + TOK * distance

        @pl.when(key0 >= TOK)
        def _(dkv=dkv):
            dkv[...] = jnp.zeros_like(dkv)

        @pl.when(key0 < TOK)
        def _(kv=kv, dkv=dkv, key0=key0):
            live = lax.broadcasted_iota(jnp.int32, (TOK, 1), 0) >= key0
            held[...] = jnp.where(live, kv[...], 0)
            acc[...] = jnp.zeros_like(acc)
            for low in range(0, TOK, TILE):
                reached = key0 < low + TILE
                if low:
                    reached &= key0 >= low

                @pl.when(reached)
                def _(low=low):
                    part(low)

            dkv[:, :HD] = jnp.where(live, acc[:, :HD] * SCALE, 0.0).astype(dkv.dtype)
            dkv[:, HD:] = jnp.where(live, acc[:, HD:], 0.0).astype(dkv.dtype)


def layout_kernel(first_ref, lengths, q, g, lse, delta, kv, *refs):
    starts, qs, gs, own_lse, far_lse, row_delta, dq, again = refs
    again[...] = kv[...]
    dq[...] = jnp.zeros_like(dq)
    count = lengths.shape[1]
    row = lax.broadcasted_iota(jnp.int32, (count, count), 0)
    col = lax.broadcasted_iota(jnp.int32, (count, count), 1)
    ends = jnp.sum(jnp.where(col <= row, lengths[...], 0), axis=1, keepdims=True)
    first = first_ref[0]
    pos = first + lax.broadcasted_iota(jnp.int32, (1, TOK), 1)
    begin = jnp.max(jnp.where(ends <= pos, ends, 0), axis=0, keepdims=True) - first
    starts[...] = begin
    for n in range(TOK // TILE):
        rows = slice(n * TILE, (n + 1) * TILE)
        for h in range(HEADS):
            hd = slice(h * HD, (h + 1) * HD)
            to = slice(n * WIDE + h * TILE, n * WIDE + (h + 1) * TILE)
            qs[to, :] = q[rows, hd]
            gs[to, :] = g[rows, hd]
            l2 = lse[h : h + 1, rows] * LOG2E
            own_lse[:, to] = l2
            far_lse[:, to] = jnp.where(begin[:, rows] <= 0, l2, FAR)
            row_delta[:, to] = delta[h : h + 1, rows]


def own_kernel(qs, gs, lse, delta, starts, kv, dq_in, dq, dkv, bias):
    begin = starts[...]
    at = lax.broadcasted_iota(jnp.int32, (TOK, TOK), 0)
    to = lax.broadcasted_iota(jnp.int32, (TOK, TOK), 1)
    bias[...] = jnp.where((at <= to) & (at >= begin), 0.0, -FAR)
    dkv[...] = jnp.zeros_like(dkv)
    for n in range(TOK // TILE):
        rows = slice(n * TILE, (n + 1) * TILE)
        wide = slice(n * WIDE, (n + 1) * WIDE)
        high = (n + 1) * TILE
        key = kv[:high, :HD]
        mask = jnp.concatenate([bias[:high, rows]] * HEADS, axis=1)
        s = dot(key, qs[wide, :], NT)
        p = jnp.exp2(s * (SCALE * LOG2E) - lse[:, wide] + mask)
        ds = p * (dot(kv[:high, HD:], gs[wide, :], NT) - delta[:, wide])
        p = p.astype(jnp.bfloat16)
        ds = ds.astype(jnp.bfloat16)
        dq[:, wide] = dq_in[:, wide] + dot(key.T, ds, NN)
        dkv[:high, :HD] += dot(ds, qs[wide, :], NN)
        dkv[:high, HD:] += dot(p, gs[wide, :], NN)
    dkv[:, :HD] = dkv[:, :HD] * SCALE


def turn_kernel(dq, *refs):
    dq_out = refs[-1]
    for n in range(TOK // TILE):
        for h in range(HEADS):
            block = dq[:, n * WIDE + h * TILE : n * WIDE + (h + 1) * TILE]
            dq_out[n * TILE : (n + 1) * TILE, h * HD : (h + 1) * HD] = (block * SCALE).T.astype(dq_out.dtype)


def finish_kernel(own, b1, b2, b3, b4, dk_out, dv_out):
    total = own[...]
    for b in (b1, b2, b3, b4):
        total = total + b[...].astype(jnp.float32)
    dk_out[...] = total[:, :HD].astype(dk_out.dtype)
    dv_out[...] = total[:, HD:].astype(dv_out.dtype)


def params(**more):
    return pltpu.CompilerParams(vmem_limit_bytes=24 << 20, **more)


EARLY = (1,)
LATE = (2, 3, 4)
GROUPS = (((1, 2), (), 2000000000), ((3, 4), (), 2000000000))
LAST = (1, 2)
COST = pl.CostEstimate(flops=2 * 10**9, bytes_accessed=0, transcendentals=0)
FIRST = pl.CostEstimate(flops=10**10, bytes_accessed=0, transcendentals=0)


def shards(query_rows, key_rows, value_rows, out_grad, logsumexp, row_delta, doc_lengths):
    bf, f32 = jnp.bfloat16, jnp.float32
    shape = jax.ShapeDtypeStruct
    first = (lax.axis_index(AXES) * TOK).astype(jnp.int32).reshape(1)
    kv = pl.pallas_call(
        pack_kernel,
        out_shape=vmem(shape((TOK, 2 * HD), bf)),
        in_specs=[HB] * 2,
        out_specs=VM,
        scratch_shapes=[pltpu.SemaphoreType.DMA((2,))],
        compiler_params=params(),
        cost_estimate=FIRST,
        name="pack",
    )(hbm(key_rows), hbm(value_rows))
    arrived = {d: shift(kv, d) for d in EARLY}
    dq_shape = shape((HD, HEADS * TOK), f32)
    row = vmem(shape((1, HEADS * TOK), f32))
    starts, query, grad, own_lse, lse, delta, dq, again = pl.pallas_call(
        layout_kernel,
        out_shape=[
            vmem(shape((1, TOK), jnp.int32)),
            vmem(shape((HEADS * TOK, HD), bf)),
            vmem(shape((HEADS * TOK, HD), bf)),
            row,
            row,
            row,
            vmem(dq_shape),
            vmem(shape((TOK, 2 * HD), bf)),
        ],
        in_specs=[SM] + [VM] * 6,
        out_specs=[VM] * 8,
        compiler_params=params(),
        cost_estimate=COST,
        name="layout",
    )(first, doc_lengths.reshape(1, -1), query_rows, out_grad, logsumexp, row_delta, kv)
    for d in LATE:
        arrived[d] = shift(again, d)
    returned = {}
    for group, tokens, flops in GROUPS:
        n = len(group)
        extra = [returned[d] for d in tokens]
        dq, *parts = pl.pallas_call(
            functools.partial(cross_kernel, group, len(extra)),
            out_shape=[vmem(dq_shape)] + [vmem(shape((TOK, 2 * HD), bf))] * n,
            in_specs=[VM] * (6 + n) + [ANY] * len(extra),
            out_specs=[VM] * (1 + n),
            scratch_shapes=[pltpu.VMEM((TOK, 2 * HD), bf), pltpu.VMEM((TOK, 2 * HD), f32)],
            input_output_aliases={5 + n: 0},
            compiler_params=params(),
            cost_estimate=pl.CostEstimate(flops=flops, bytes_accessed=0, transcendentals=0),
            name="cross" + "".join(str(d) for d in group),
        )(query, grad, lse, delta, starts, *[arrived[d] for d in group], dq, *extra)
        for d, array in zip(group, parts):
            returned[d] = shift(array, -d)
    dq, own = pl.pallas_call(
        own_kernel,
        out_shape=[vmem(dq_shape), vmem(shape((TOK, 2 * HD), f32))],
        in_specs=[VM] * 7,
        out_specs=[VM] * 2,
        scratch_shapes=[pltpu.VMEM((TOK, TOK), f32)],
        input_output_aliases={6: 0},
        compiler_params=params(),
        cost_estimate=COST,
        name="own",
    )(query, grad, own_lse, delta, starts, kv, dq)
    tokens = [returned[d] for d in LAST]
    query_grad = pl.pallas_call(
        turn_kernel,
        out_shape=shape((TOK, HEADS * HD), bf),
        in_specs=[VM] + [ANY] * len(tokens),
        out_specs=VM,
        compiler_params=params(),
        cost_estimate=COST,
        name="turn",
    )(dq, *tokens)
    key_grad, value_grad = pl.pallas_call(
        finish_kernel,
        out_shape=[shape((TOK, HD), bf)] * 2,
        in_specs=[VM] * 5,
        out_specs=[VM] * 2,
        compiler_params=params(),
        cost_estimate=COST,
        name="finish",
    )(own, *[returned[d] for d in range(1, REACH + 1)])
    return query_grad, key_grad, value_grad


def solution(mesh):
    rows = P(AXES, None)
    return jax.shard_map(
        shards,
        mesh=mesh,
        in_specs=(rows, rows, rows, rows, P(None, AXES), P(None, AXES), P()),
        out_specs=(rows, rows, rows),
        check_vma=False,
    )
```
